32 devices in a mesh: member: 2 (over y), band: 16 (over z, x, core).
Axes of the slice: x: 2, y: 2, z: 4, core: 2. Of those that a mesh axis runs over, the one named last changes fastest.
Arguments:
- grid_latent: bfloat16 [16384, 512], P(('member', 'band')), parts along dimension 0, may hold values from -6 to 6
- mesh_latent: bfloat16 [10240, 512], P(('member', 'band')), parts along dimension 0, may hold values from -6 to 6
- g2m_latent: bfloat16 [24576, 512], P(('member', 'band')), parts along dimension 0, may hold values from -6 to 6
- edge_latent: bfloat16 [32768, 512], P(('member', 'band')), parts along dimension 0, may hold values from -6 to 6
- cotangent: bfloat16 [10240, 512], P(('member', 'band')), parts along dimension 0, may hold values from -8 to 8
- grid_send: int32 [16, 32], P('band'), may hold values from 0 to 511
- g2m_sender: int32 [12288], P('band'), may hold values from 0 to 543
- g2m_receiver: int32 [12288], P('band'), may hold values from 0 to 319
- node_send: int32 [16, 32], P('band'), may hold values from 0 to 319
- edge_sender: int32 [16384], P('band'), may hold values from 0 to 351
- edge_receiver: int32 [16384], P('band'), may hold values from 0 to 319
- edge_count: int32 [16], P('band'), may hold values from 1 to 1023, as said below
- enc_edge_in: bfloat16 [1536, 512], replicated, may hold values from -0.15625 to 0.15625
- enc_edge_out: bfloat16 [512, 512], replicated, may hold values from -0.25 to 0.25
- enc_node_in: bfloat16 [1024, 512], replicated, may hold values from -0.1875 to 0.1875
- enc_node_out: bfloat16 [512, 512], replicated, may hold values from -0.25 to 0.25
- proc_edge_in: bfloat16 [1536, 512], replicated, may hold values from -0.15625 to 0.15625
- proc_edge_out: bfloat16 [512, 512], replicated, may hold values from -0.25 to 0.25
- proc_node_in: bfloat16 [1024, 512], replicated, may hold values from -0.1875 to 0.1875
- proc_node_out: bfloat16 [512, 512], replicated, may hold values from -0.25 to 0.25
- norm_gains: float32 [4, 512], replicated, may hold values from 0.5 to 1.5
- norm_biases: float32 [4, 512], replicated, may hold values from -0.5 to 0.5
Outputs:
- mesh_out: bfloat16 [10240, 512], P(('member', 'band')), parts along dimension 0
- grad_mesh: float32 [10240, 512], P(('member', 'band')), parts along dimension 0
- grad_edge_in: float32 [3072, 512], P('member', 'band'), parts along dimension 0
- grad_edge_out: float32 [1024, 512], P('member', 'band'), parts along dimension 0
- grad_node_in: float32 [2048, 512], P('member', 'band'), parts along dimension 0
- grad_node_out: float32 [1024, 512], P('member', 'band'), parts along dimension 0
The draws below stay inside these ranges and needn't reach their ends.
There are 2 independent parts, one for each index of `member`. The reference program is written for one: setup_inputs(seed, part) draws one part's arguments, and reference() takes and returns one part's arrays. A program takes and returns all parts, laid end to end along the dimension named above; an argument that names none is the same for every part. Nothing has to cross between parts.
Inputs may be any that keep to these rules, and one draw needn't show every extreme that they name: Device i's live mesh edges are its slots 0 to edge_count[i] - 1. For i < 8, devices i and i + 8 together hold at most 1024 live edges, and exactly that many in at least one such pair.
All inputs are finite; a program needn't handle non-finite values.
Results may differ from the reference program's by a relative error of at most 0.015.
Values may be sent and summed in bfloat16 or wider, within the bound.
A program may use at most 128 MiB of HBM per device.

```python
import jax
import jax.numpy as jnp
from jax import lax

LAT = 512
NODE_DEV = 320
GRID_DEV = 512
G2M_DEV = 768
EDGE_CAP = 1024
HSLOT = 2
GSLOT = 2
MESH_NODES = 5120
GRIDS = 8192
G2M = 12288
EDGES = 16384
HTAB = 352
GTAB = 544
N_BAND = 16


def draw_edge_count(key, part):
    key = jax.random.fold_in(key, 11)
    pair_count = N_BAND // 2
    key_forced, key_total, key_first = jax.random.split(key, 3)
    forced = jax.random.randint(key_forced, (), 0, pair_count)
    totals = jax.random.randint(key_total, (pair_count,), EDGE_CAP // 2, EDGE_CAP + 1)
    firsts = 1 + jax.random.randint(key_first, (pair_count,), 0, EDGE_CAP) % (totals - 1)
    pair_ids = jnp.arange(pair_count)
    totals = jnp.where(pair_ids == forced, EDGE_CAP, totals)
    firsts = jnp.where(pair_ids == forced, EDGE_CAP - 1, firsts)
    return jnp.concatenate([firsts, totals - firsts]).astype(jnp.int32)


def plant(result, key, smallest, high):
    index_at = [jax.random.randint(jax.random.fold_in(key, axis), (), 0, length) for axis, length in enumerate(result.shape)]
    widest = result.shape.index(max(result.shape))
    next_to = index_at[:widest] + [(index_at[widest] + 1) % result.shape[widest]] + index_at[widest + 1:]
    return result.at[tuple(index_at)].set(smallest).at[tuple(next_to)].set(high)


def with_spikes(entries, stream_key, source, target, shards_of, factor):
    def block_of(axis_at):
        return (jnp.arange(entries.shape[axis_at]) // (entries.shape[axis_at] // shards_of)).reshape((-1,) + (1,) * (entries.ndim - 1 - axis_at))

    near = jax.random.permutation(stream_key, shards_of)[block_of(target)]
    second = (block_of(target) + shards_of // 2) % shards_of
    return jnp.where((block_of(source) == near) | (block_of(source) == second), factor * entries, entries)


def steps_of(rng, shape, shards, smallest, high):
    def one(dim, parts):
        draws = jax.random.uniform(jax.random.fold_in(jax.random.fold_in(rng, 6), dim), (parts,), jnp.float32, smallest / len(shards), high / len(shards))
        return jnp.repeat(jnp.exp(draws), shape[dim] // parts).reshape((-1,) + (1,) * (len(shape) - dim - 1))

    loudness = one(*shards[0])
    for cut in shards[1:]:
        loudness = loudness * one(*cut)
    return loudness


def bell_draw(key, extent, width, limit, cuts=(), held_as=jnp.bfloat16):
    drawn = jax.random.normal(key, extent, jnp.float32) * width
    if len(cuts) > 0:
        drawn = steps_of(key, extent, cuts, -0.22, 0.18) * drawn
    return jnp.clip(drawn, min=-limit, max=limit).astype(held_as)


def noise_with(rng, shape, spread, reach, cuts, heavy, held_as=jnp.bfloat16):
    drawn = spread * jax.random.normal(rng, shape, jnp.float32)
    if cuts:
        drawn = drawn * steps_of(rng, shape, cuts, -0.22, 0.18)
    return jnp.clip(with_spikes(drawn, jax.random.fold_in(rng, 3), *heavy), -reach, reach).astype(held_as)


def setup_inputs(seed: int = 0, part: int = 0) -> dict:
    splits = jax.random.split(jax.random.key(seed), 23)
    own_keys = jax.random.split(jax.random.fold_in(splits[22], part), 23)
    return {
        "grid_latent": bell_draw(own_keys[0], (GRIDS, LAT), 1.0, 6.0, ((0, 16),)),
        "mesh_latent": bell_draw(own_keys[1], (MESH_NODES, LAT), 1.0, 6.0, ((0, 16),)),
        "g2m_latent": bell_draw(own_keys[2], (G2M, LAT), 1.0, 6.0, ((0, 16),)),
        "edge_latent": bell_draw(own_keys[3], (EDGES, LAT), 1.0, 6.0, ((0, 16),)),
        "cotangent": noise_with(own_keys[4], (MESH_NODES, LAT), 1.0, 8.0, ((0, 16),), (0, 1, 16, 2.0)),
        "grid_send": plant(jax.random.randint(splits[5], (N_BAND, N_BAND * GSLOT), 0, GRID_DEV), jax.random.fold_in(splits[5], 1), 0, GRID_DEV - 1).astype(jnp.int32),
        "g2m_sender": plant(jax.random.randint(splits[6], (G2M,), 0, GTAB), jax.random.fold_in(splits[6], 1), 0, GTAB - 1).astype(jnp.int32),
        "g2m_receiver": plant(jax.random.randint(splits[7], (G2M,), 0, NODE_DEV), jax.random.fold_in(splits[7], 1), 0, NODE_DEV - 1).astype(jnp.int32),
        "node_send": plant(jax.random.randint(splits[8], (N_BAND, N_BAND * HSLOT), 0, NODE_DEV), jax.random.fold_in(splits[8], 1), 0, NODE_DEV - 1).astype(jnp.int32),
        "edge_sender": plant(jax.random.randint(splits[9], (EDGES,), 0, HTAB), jax.random.fold_in(splits[9], 1), 0, HTAB - 1).astype(jnp.int32),
        "edge_receiver": plant(jax.random.randint(splits[10], (EDGES,), 0, NODE_DEV), jax.random.fold_in(splits[10], 1), 0, NODE_DEV - 1).astype(jnp.int32),
        "edge_count": draw_edge_count(jax.random.fold_in(splits[22], 71), part),
        "enc_edge_in": bell_draw(splits[12], (3 * LAT, LAT), (3 * LAT) ** -0.5, 0.15625),
        "enc_edge_out": bell_draw(splits[13], (LAT, LAT), LAT ** -0.5, 0.25),
        "enc_node_in": bell_draw(splits[14], (2 * LAT, LAT), (2 * LAT) ** -0.5, 0.1875),
        "enc_node_out": bell_draw(splits[15], (LAT, LAT), LAT ** -0.5, 0.25),
        "proc_edge_in": bell_draw(splits[16], (3 * LAT, LAT), (3 * LAT) ** -0.5, 0.15625),
        "proc_edge_out": bell_draw(splits[17], (LAT, LAT), LAT ** -0.5, 0.25),
        "proc_node_in": bell_draw(splits[18], (2 * LAT, LAT), (2 * LAT) ** -0.5, 0.1875),
        "proc_node_out": bell_draw(splits[19], (LAT, LAT), LAT ** -0.5, 0.25),
        "norm_gains": jnp.clip(1.0 + 0.1 * jax.random.normal(splits[20], (4, LAT), jnp.float32), 0.5, 1.5),
        "norm_biases": jnp.clip(jax.random.uniform(splits[21], (4, LAT), jnp.float32, -0.5, 0.5), -0.5, 0.5),
    }


EPS = 1e-05

def layer_norm(linear, gain_row, bias_row):
    average = lax.optimization_barrier(jnp.mean(linear, axis=-1, keepdims=True))
    centred = linear - average
    inverse = lax.rsqrt(lax.optimization_barrier(jnp.mean(centred * centred, axis=-1, keepdims=True)) + EPS)
    return centred * inverse * gain_row + bias_row

def norm_back(linear, gain_row, upstream):
    average = lax.optimization_barrier(jnp.mean(linear, axis=-1, keepdims=True))
    centred = linear - average
    inverse = lax.rsqrt(lax.optimization_barrier(jnp.mean(centred * centred, axis=-1, keepdims=True)) + EPS)
    normed = centred * inverse
    scaled = upstream * gain_row
    return inverse * (scaled - lax.optimization_barrier(jnp.mean(scaled, axis=-1, keepdims=True)) - normed * lax.optimization_barrier(jnp.mean(scaled * normed, axis=-1, keepdims=True)))

def silu_slope(preact):
    sigmoid_val = jax.nn.sigmoid(preact)
    return sigmoid_val * (1.0 + preact * (1.0 - sigmoid_val))

def dense_pass(inputs, weight_in, weight_out, gain_row, bias_row):
    preact = jnp.dot(inputs, weight_in, preferred_element_type=jnp.float32)
    hidden = jax.nn.silu(preact).astype(jnp.bfloat16)
    linear = jnp.dot(hidden, weight_out, preferred_element_type=jnp.float32)
    return (preact, hidden, linear, layer_norm(linear, gain_row, bias_row))

def one_hot(indices, rows_total):
    return (indices[None, :] == jnp.arange(rows_total, dtype=jnp.int32)[:, None]).astype(jnp.bfloat16)

def remote_rows(flat_rows, send_table, per_device, slot_count):
    blocks = send_table.reshape(N_BAND, N_BAND, slot_count)
    global_ids = jnp.arange(N_BAND, dtype=jnp.int32)[:, None, None] * per_device + blocks
    gathered = jnp.take(flat_rows, global_ids.reshape(-1).astype(jnp.int32), axis=0)
    gathered = gathered.reshape(N_BAND, N_BAND, slot_count, LAT)
    return jnp.transpose(gathered, (1, 0, 2, 3)).reshape(N_BAND, N_BAND * slot_count, LAT)

def reference(grid_latent, mesh_latent, g2m_latent, edge_latent, cotangent, grid_send, g2m_sender, g2m_receiver, node_send, edge_sender, edge_receiver, edge_count, enc_edge_in, enc_edge_out, enc_node_in, enc_node_out, proc_edge_in, proc_edge_out, proc_node_in, proc_node_out, norm_gains, norm_biases):
    grid_blocks = grid_latent.reshape(N_BAND, GRID_DEV, LAT)
    mesh_blocks = mesh_latent.reshape(N_BAND, NODE_DEV, LAT)
    grid_tables = jnp.concatenate([grid_blocks, remote_rows(grid_latent, grid_send, GRID_DEV, GSLOT)], axis=1)

    def encode(device_args):
        grid_table, nodes, edge_rows, senders, receivers = device_args
        enc_inputs = jnp.concatenate([jnp.take(grid_table, senders, axis=0), jnp.take(nodes, receivers, axis=0), edge_rows], axis=1)
        enc_message = dense_pass(enc_inputs, enc_edge_in, enc_edge_out, norm_gains[0], norm_biases[0])[3].astype(jnp.bfloat16)
        enc_sum = jnp.dot(one_hot(receivers, NODE_DEV), enc_message, preferred_element_type=jnp.float32).astype(jnp.bfloat16)
        update = dense_pass(jnp.concatenate([nodes, enc_sum], axis=1), enc_node_in, enc_node_out, norm_gains[1], norm_biases[1])[3]
        return (nodes.astype(jnp.float32) + update).astype(jnp.bfloat16)
    encoded = lax.map(encode, (grid_tables, mesh_blocks, g2m_latent.reshape(N_BAND, G2M_DEV, LAT), g2m_sender.reshape(N_BAND, G2M_DEV), g2m_receiver.reshape(N_BAND, G2M_DEV)))
    node_tables = jnp.concatenate([encoded, remote_rows(encoded.reshape(MESH_NODES, LAT), node_send, NODE_DEV, HSLOT)], axis=1)

    def process(totals, device_args):
        node_table, nodes, edge_rows, senders, receivers, live_count, upstream_rows = device_args
        live_mask = (jnp.arange(EDGE_CAP, dtype=jnp.int32) < live_count).astype(jnp.float32)[:, None]
        inputs = jnp.concatenate([jnp.take(node_table, senders, axis=0), jnp.take(nodes, receivers, axis=0), edge_rows], axis=1)
        preact, hidden, linear, normed = dense_pass(inputs, proc_edge_in, proc_edge_out, norm_gains[2], norm_biases[2])
        message = (normed * live_mask).astype(jnp.bfloat16)
        recv_hot = one_hot(receivers, NODE_DEV)
        proc_sum = jnp.dot(recv_hot, message, preferred_element_type=jnp.float32).astype(jnp.bfloat16)
        node_in = jnp.concatenate([nodes, proc_sum], axis=1)
        node_pre, node_hidden, node_linear, node_normed = dense_pass(node_in, proc_node_in, proc_node_out, norm_gains[3], norm_biases[3])
        mesh_rows = (nodes.astype(jnp.float32) + node_normed).astype(jnp.bfloat16)
        upstream = upstream_rows.astype(jnp.float32)
        node_lin_grad = norm_back(node_linear, norm_gains[3], upstream).astype(jnp.bfloat16)
        node_out_term = jnp.dot(node_hidden.T, node_lin_grad, preferred_element_type=jnp.float32)
        node_pre_grad = (jnp.dot(node_lin_grad, proc_node_out.T, preferred_element_type=jnp.float32) * silu_slope(node_pre)).astype(jnp.bfloat16)
        node_in_term = jnp.dot(node_in.T, node_pre_grad, preferred_element_type=jnp.float32)
        node_in_grad = jnp.dot(node_pre_grad, proc_node_in.T, preferred_element_type=jnp.float32)
        sum_grad = node_in_grad[:, LAT:].astype(jnp.bfloat16)
        msg_grad = jnp.take(sum_grad, receivers, axis=0).astype(jnp.float32) * live_mask
        edge_lin_grad = norm_back(linear, norm_gains[2], msg_grad).astype(jnp.bfloat16)
        edge_out_term = jnp.dot(hidden.T, edge_lin_grad, preferred_element_type=jnp.float32)
        edge_pre_grad = (jnp.dot(edge_lin_grad, proc_edge_out.T, preferred_element_type=jnp.float32) * silu_slope(preact)).astype(jnp.bfloat16)
        edge_in_term = jnp.dot(inputs.T, edge_pre_grad, preferred_element_type=jnp.float32)
        input_grad = jnp.dot(edge_pre_grad, proc_edge_in[:2 * LAT].T, preferred_element_type=jnp.float32).astype(jnp.bfloat16)
        table_grad = jnp.dot(one_hot(senders, HTAB), input_grad[:, :LAT], preferred_element_type=jnp.float32)
        recv_grad = jnp.dot(recv_hot, input_grad[:, LAT:], preferred_element_type=jnp.float32)
        local_grad = upstream + node_in_grad[:, :LAT] + recv_grad + table_grad[:NODE_DEV]
        slot_grad = table_grad[NODE_DEV:].astype(jnp.bfloat16)
        totals = (totals[0] + edge_in_term, totals[1] + edge_out_term, totals[2] + node_in_term, totals[3] + node_out_term)
        return (totals, (mesh_rows, local_grad, slot_grad))
    start = (jnp.zeros((3 * LAT, LAT), jnp.float32), jnp.zeros((LAT, LAT), jnp.float32), jnp.zeros((2 * LAT, LAT), jnp.float32), jnp.zeros((LAT, LAT), jnp.float32))
    totals, (mesh_rows, local_grads, slot_grads) = lax.scan(process, start, (node_tables, encoded, edge_latent.reshape(N_BAND, EDGE_CAP, LAT), edge_sender.reshape(N_BAND, EDGE_CAP), edge_receiver.reshape(N_BAND, EDGE_CAP), edge_count, cotangent.reshape(N_BAND, NODE_DEV, LAT)))
    returned = jnp.transpose(slot_grads.reshape(N_BAND, N_BAND, HSLOT, LAT), (1, 0, 2, 3))
    returned = returned.reshape(N_BAND, N_BAND * HSLOT, LAT)

    def add_back(device_args):
        send_row, returned_rows = device_args
        return jnp.dot(one_hot(send_row, NODE_DEV), returned_rows, preferred_element_type=jnp.float32)
    extra = lax.map(add_back, (node_send, returned))
    grad_mesh = (local_grads + extra).reshape(MESH_NODES, LAT)
    edge_scale = 1.0 / EDGES ** 0.5
    node_scale = 1.0 / MESH_NODES ** 0.5
    return (mesh_rows.reshape(MESH_NODES, LAT), grad_mesh, totals[0] * edge_scale, totals[1] * edge_scale, totals[2] * node_scale, totals[3] * node_scale)
```

```python
import functools

import jax
import jax.numpy as jnp
from jax import lax
from jax.experimental import pallas as pl
from jax.experimental.pallas import tpu as pltpu
from jax.sharding import PartitionSpec as P

EPS = 1e-05
F32 = jnp.float32
BF16 = jnp.bfloat16
UNITS = 7
LANE = 128


def round_up(value, step):
    return (value + step - 1) // step * step


def nn(a, b):
    return jnp.dot(a, b, preferred_element_type=F32)


def nt(a, b):
    return lax.dot_general(a, b, (((1,), (1,)), ((), ())), preferred_element_type=F32)


def tn(a, b):
    return lax.dot_general(a, b, (((0,), (0,)), ((), ())), preferred_element_type=F32)


def sigmoid(a):
    return 0.5 * jnp.tanh(0.5 * a) + 0.5


def silu_slope(a):
    s = sigmoid(a)
    return s * (1.0 + a * (1.0 - s))


def normalise(linear):
    centred = linear - jnp.mean(linear, axis=-1, keepdims=True)
    inverse = lax.rsqrt(jnp.mean(centred * centred, axis=-1, keepdims=True) + EPS)
    return centred * inverse, inverse


def norm_back(z, inverse, scaled):
    return inverse * (
        scaled
        - jnp.mean(scaled, axis=-1, keepdims=True)
        - z * jnp.mean(scaled * z, axis=-1, keepdims=True)
    )


def hot_rows(index_row, rows_total, first=0):
    edges = index_row.shape[1]
    ids = lax.broadcasted_iota(jnp.int32, (rows_total, edges), 0) + first
    return jnp.where(ids == index_row, 1.0, 0.0).astype(BF16)


def over_lanes(index_row):
    edges = index_row.shape[1]
    return jnp.transpose(jnp.broadcast_to(index_row.astype(F32), (LANE, edges)))


def hot_pair(sender_row, receiver_row, split, total):
    edges = sender_row.shape[1]
    ids = lax.broadcasted_iota(jnp.int32, (edges, LANE), 1).astype(F32)
    senders, receivers = over_lanes(sender_row), over_lanes(receiver_row)
    blocks = []
    for start in range(0, total, LANE):
        held = senders if start < split else receivers
        offset = start if start < split else start - split
        blocks.append(jnp.where(held == ids + float(offset), 1.0, 0.0).astype(BF16))
    return jnp.concatenate(blocks, axis=1)


def kernel(n, inside, sizes, *refs):
    (grid_rows, nodes, enc_edges, slots_total, lat, tile, halo, split_enc, total_enc, split_proc, total_proc) = sizes
    stages = n.bit_length() - 1
    refs = list(refs)
    hbm = refs[:13]
    (count_ref, gsend_col, nsend_col, nsend_row, g2m_s, g2m_r, edge_s, edge_r, gains, biases) = refs[13:23]
    mesh_out_ref, grad_mesh_ref, grads_ref = refs[23:26]
    vm = refs[26:39]
    (table_enc, table_proc, node_table, acc_node, pre_ref, z_ref, inv_ref, hid_ref, elg_ref, epg_ref,
     sum_ref, upd_ref, a_send, a_recv, in_sem, a_ssem, a_rsem) = refs[39:56]
    rest = refs[56:]
    if inside:
        full_ref, keep, send, recv, r_ssem, r_rsem = (
            rest[0], rest[1:1 + stages], rest[1 + stages:1 + 2 * stages], rest[1 + 2 * stages:1 + 3 * stages],
            rest[1 + 3 * stages], rest[2 + 3 * stages])
    else:
        full_ref = grads_ref
    me = lax.axis_index("band")

    barrier = pltpu.get_barrier_semaphore()

    def greet(step, carry):
        pl.semaphore_signal(barrier, inc=1, device_id={"band": lax.rem(me + step, n)}, device_id_type=pl.DeviceIdType.MESH)
        return carry

    copies = [pltpu.make_async_copy(hbm[i], vm[i], in_sem.at[i]) for i in range(13)]
    (GRID, MESH, G2M, EDGE, COT, EEI, EEO, ENI, ENO, PEI, PEO, PNI, PNO) = range(13)
    for i in (GRID, EEI, MESH, G2M, EEO, ENI, ENO, PEI, EDGE, PEO, PNI, PNO, COT):
        copies[i].start()
    lax.fori_loop(1, n, greet, 0)

    rows_block = halo * lat // LANE // n
    spread = lat // LANE

    def exchange_start(which, rows):
        for c in range(spread):
            a_send[which, pl.ds(c, halo, stride=spread), :] = rows[:, c * LANE:(c + 1) * LANE]
        own = pl.ds(pl.multiple_of(me * rows_block, rows_block), rows_block)
        a_recv[which, own, :] = a_send[which, own, :]

        def go(step, carry):
            peer = lax.rem(me + step, n)
            pltpu.make_async_remote_copy(
                src_ref=a_send.at[which, pl.ds(pl.multiple_of(peer * rows_block, rows_block), rows_block)],
                dst_ref=a_recv.at[which, own],
                send_sem=a_ssem.at[which],
                recv_sem=a_rsem.at[which],
                device_id={"band": peer},
                device_id_type=pl.DeviceIdType.MESH,
            ).start()
            return carry

        lax.fori_loop(1, n, go, 0)

    def exchange_wait(which):
        most = pl.ds(0, (n - 1) * rows_block)
        pltpu.make_async_copy(a_send.at[which, most], a_recv.at[which, most], a_rsem.at[which]).wait()
        pltpu.make_async_copy(a_send.at[which, most], a_recv.at[which, most], a_ssem.at[which]).wait()
        return jnp.concatenate([a_recv[which, pl.ds(c, halo, stride=spread), :] for c in range(spread)], axis=1).astype(BF16)

    block = lat // n
    if inside:
        bits = [lax.rem(lax.div(me, jnp.int32(1 << k)), jnp.int32(2)) for k in range(stages)]

    def remote(units, k):
        first, count = units
        return pltpu.make_async_remote_copy(
            src_ref=send[k].at[pl.ds(first, count)],
            dst_ref=recv[k].at[pl.ds(first, count)],
            send_sem=r_ssem.at[first, k],
            recv_sem=r_rsem.at[first, k],
            device_id={"band": me + (1 - 2 * bits[k]) * (1 << k)},
            device_id_type=pl.DeviceIdType.MESH,
        )

    def reduce_step(units, k):
        if not inside:
            return
        first, count = units
        us = pl.ds(first, count)

        def value(j):
            rows = pl.ds(pl.multiple_of(j * block, block), block)
            if k == 0:
                return full_ref[us, rows, :]
            return keep[k - 1][us, rows, :] + recv[k - 1][us, rows, :].astype(F32)

        if k > 0:
            remote(units, k - 1).wait_recv()
        if k == stages:
            grads_ref[us, :, :] = value(0)
            return
        for j in range(n >> (k + 1)):
            send[k][us, j * block:(j + 1) * block, :] = value(2 * j + 1 - bits[k]).astype(BF16)
        remote(units, k).start()
        for j in range(n >> (k + 1)):
            keep[k][us, j * block:(j + 1) * block, :] = value(2 * j + bits[k])

    NODE, EOUT, EA, EB = (0, 3), (3, 1), (6, 1), (4, 2)

    copies[GRID].wait()
    grid = vm[GRID]
    ids = lax.broadcasted_iota(jnp.int32, (halo, grid_rows), 1)
    outgoing = nn(jnp.where(ids == gsend_col[...], 1.0, 0.0).astype(BF16), grid[...])
    pl.semaphore_wait(barrier, n - 1)
    exchange_start(0, outgoing)
    copies[EEI].wait()
    copies[MESH].wait()
    eei = vm[EEI]
    mesh = vm[MESH]
    table_enc[0:grid_rows, :] = nn(grid[...], eei[0:lat, :]).astype(BF16)
    table_enc[split_enc:split_enc + nodes, :] = nn(mesh[...], eei[lat:2 * lat, :]).astype(BF16)
    if split_enc > grid_rows + halo:
        table_enc[grid_rows + halo:split_enc, :] = jnp.zeros((split_enc - grid_rows - halo, lat), BF16)
    if total_enc > split_enc + nodes:
        table_enc[split_enc + nodes:total_enc, :] = jnp.zeros((total_enc - split_enc - nodes, lat), BF16)
    if split_proc > nodes + halo:
        table_proc[nodes + halo:split_proc, :] = jnp.zeros((split_proc - nodes - halo, lat), BF16)
    if total_proc > split_proc + nodes:
        table_proc[split_proc + nodes:total_proc, :] = jnp.zeros((total_proc - split_proc - nodes, lat), BF16)
    copies[G2M].wait()
    copies[EEO].wait()
    copies[ENI].wait()
    acc_node[...] = jnp.zeros_like(acc_node)
    upd_ref[...] = nn(mesh[...], vm[ENI][0:lat, :])
    arrived = exchange_wait(0)
    table_enc[grid_rows:grid_rows + halo, :] = nn(arrived, eei[0:lat, :]).astype(BF16)

    def encode(t, carry):
        rows = pl.ds(pl.multiple_of(t * tile, tile), tile)
        receivers = g2m_r[t]
        pre = nn(hot_pair(g2m_s[t], receivers, split_enc, total_enc), table_enc[...])
        pre = pre + nn(vm[G2M][rows, :], eei[2 * lat:3 * lat, :])
        hidden = (pre * sigmoid(pre)).astype(BF16)
        z, _ = normalise(nn(hidden, vm[EEO][...]))
        message = (z * gains[0:1, :] + biases[0:1, :]).astype(BF16)
        acc_node[...] += nn(hot_rows(receivers, nodes), message)
        return carry

    lax.fori_loop(0, enc_edges // tile, encode, 0)
    copies[ENO].wait()
    pre = upd_ref[...] + nn(acc_node[...].astype(BF16), vm[ENI][lat:2 * lat, :])
    hidden = (pre * sigmoid(pre)).astype(BF16)
    z, _ = normalise(nn(hidden, vm[ENO][...]))
    encoded = (mesh[...].astype(F32) + z * gains[1:2, :] + biases[1:2, :]).astype(BF16)
    node_table[0:nodes, :] = encoded
    ids = lax.broadcasted_iota(jnp.int32, (halo, nodes), 1)
    exchange_start(1, nn(jnp.where(ids == nsend_col[...], 1.0, 0.0).astype(BF16), encoded))

    copies[PEI].wait()
    copies[EDGE].wait()
    copies[PEO].wait()
    copies[PNI].wait()
    pei, pni = vm[PEI], vm[PNI]
    table_proc[0:nodes, :] = nn(encoded, pei[0:lat, :]).astype(BF16)
    table_proc[split_proc:split_proc + nodes, :] = nn(encoded, pei[lat:2 * lat, :]).astype(BF16)
    upd_ref[...] = nn(encoded, pni[0:lat, :])

    def edge_part(t, carry):
        rows = pl.ds(pl.multiple_of(t * tile, tile), tile)
        pre_ref[rows, :] = nn(vm[EDGE][rows, :], pei[2 * lat:3 * lat, :])
        return carry

    lax.fori_loop(0, slots_total // tile, edge_part, 0)
    acc_node[...] = jnp.zeros_like(acc_node)
    arrived = exchange_wait(1)
    node_table[nodes:nodes + halo, :] = arrived
    table_proc[nodes:nodes + halo, :] = nn(arrived, pei[0:lat, :]).astype(BF16)
    count = count_ref[0]

    def live_rows(ref, t):
        slot = lax.broadcasted_iota(jnp.int32, (1, tile), 1) + t * tile
        return jnp.where(slot < count, ref[t], -1)

    def process(t, carry):
        rows = pl.ds(pl.multiple_of(t * tile, tile), tile)
        receivers = live_rows(edge_r, t)
        pre = pre_ref[rows, :] + nn(hot_pair(live_rows(edge_s, t), receivers, split_proc, total_proc), table_proc[...])
        pre_ref[rows, :] = pre
        hidden = (pre * sigmoid(pre)).astype(BF16)
        hid_ref[rows, :] = hidden
        z, inverse = normalise(nn(hidden, vm[PEO][...]))
        z_ref[rows, :] = z
        inv_ref[rows, :] = jnp.broadcast_to(inverse, (tile, LANE))
        message = (z * gains[2:3, :] + biases[2:3, :]).astype(BF16)
        acc_node[...] += nn(hot_rows(receivers, nodes), message)
        return carry

    lax.fori_loop(0, slots_total // tile, process, 0)

    proc_sum = acc_node[...].astype(BF16)
    copies[PNO].wait()
    copies[COT].wait()
    pno, cot = vm[PNO], vm[COT]
    pre = upd_ref[...] + nn(proc_sum, pni[lat:2 * lat, :])
    hidden = (pre * sigmoid(pre)).astype(BF16)
    z, inverse = normalise(nn(hidden, pno[...]))
    mesh_out_ref[...] = (encoded.astype(F32) + z * gains[3:4, :] + biases[3:4, :]).astype(BF16)
    lin_grad = norm_back(z, inverse, cot[...].astype(F32) * gains[3:4, :]).astype(BF16)
    pre_grad = (nt(lin_grad, pno[...]) * silu_slope(pre)).astype(BF16)
    full_ref[0, :, :] = tn(lin_grad, hidden)
    full_ref[1, :, :] = tn(pre_grad, encoded)
    full_ref[2, :, :] = tn(pre_grad, proc_sum)
    reduce_step(NODE, 0)
    sum_grad = nt(pre_grad, pni[lat:2 * lat, :]).astype(BF16)
    grad_mesh_ref[...] = cot[...].astype(F32) + nt(pre_grad, pni[0:lat, :])
    if split_proc + nodes < total_proc:
        table_proc[split_proc + nodes:total_proc, :] = jnp.zeros((total_proc - split_proc - nodes, lat), BF16)
    table_proc[split_proc:split_proc + nodes, :] = sum_grad
    sum_ref[...] = jnp.zeros_like(sum_ref)

    def edge_back(t, carry):
        rows = pl.ds(pl.multiple_of(t * tile, tile), tile)
        senders, receivers = live_rows(edge_s, t), live_rows(edge_r, t)
        held = over_lanes(receivers)
        ids = lax.broadcasted_iota(jnp.int32, (tile, LANE), 1).astype(F32)
        hot = jnp.concatenate(
            [jnp.where(held == ids + float(s), 1.0, 0.0).astype(BF16) for s in range(0, total_proc - split_proc, LANE)], axis=1)
        upstream = nn(hot, table_proc[split_proc:total_proc, :])
        grad = norm_back(z_ref[rows, :], inv_ref[rows, 0:1], upstream * gains[2:3, :]).astype(BF16)
        elg_ref[rows, :] = grad
        grad = (nt(grad, vm[PEO][...]) * silu_slope(pre_ref[rows, :])).astype(BF16)
        epg_ref[rows, :] = grad
        sum_ref[0:split_proc, :] += nn(hot_rows(senders, split_proc), grad)
        sum_ref[split_proc:split_proc + nodes, :] += nn(hot_rows(receivers, nodes), grad)
        return carry

    half = slots_total // tile // 2
    lax.fori_loop(0, half, edge_back, 0)
    reduce_step(NODE, 1)
    lax.fori_loop(half, slots_total // tile, edge_back, 0)
    reduce_step(NODE, 2)
    by_sender = sum_ref[0:nodes + halo, :].astype(BF16)
    by_receiver = sum_ref[split_proc:split_proc + nodes, :].astype(BF16)
    exchange_start(2, nt(by_sender[nodes:nodes + halo, :], pei[0:lat, :]))
    full_ref[3, :, :] = tn(elg_ref[...], hid_ref[...])
    reduce_step(EOUT, 0)
    full_ref[6, :, :] = tn(epg_ref[...], vm[EDGE][...])
    reduce_step(EA, 0)
    reduce_step(NODE, 3)
    reduce_step(EOUT, 1)
    full_ref[4, :, :] = tn(by_sender, node_table[...])
    full_ref[5, :, :] = tn(by_receiver, node_table[0:nodes, :])
    reduce_step(EB, 0)
    reduce_step(EA, 1)
    grad_mesh_ref[...] += nt(by_sender[0:nodes, :], pei[0:lat, :]) + nt(by_receiver, pei[lat:2 * lat, :])
    reduce_step(EB, 1)
    reduce_step(EOUT, 2)
    arrived = exchange_wait(2)
    grad_mesh_ref[...] += nn(hot_rows(nsend_row[...], nodes), arrived)
    reduce_step(NODE, 4)
    reduce_step(EA, 2)
    reduce_step(EOUT, 3)
    reduce_step(EB, 2)
    reduce_step(EA, 3)
    reduce_step(EOUT, 4)
    reduce_step(EB, 3)
    reduce_step(EA, 4)
    reduce_step(EB, 4)
    if inside:
        for units in (NODE, EOUT, EA, EB):
            for k in range(stages):
                remote(units, k).wait_send()


def on_device(n, *args):
    (grid_latent, mesh_latent, g2m_latent, edge_latent, cotangent, grid_send, g2m_sender, g2m_receiver, node_send,
     edge_sender, edge_receiver, edge_count, *weights) = args
    weights, (gains, biases) = weights[:8], weights[8:]
    lat = mesh_latent.shape[1]
    grid_rows, nodes = grid_latent.shape[0], mesh_latent.shape[0]
    enc_edges, slots_total = g2m_latent.shape[0], edge_latent.shape[0]
    halo = node_send.shape[1]
    tile = 256
    inside = n == 16
    split_enc = round_up(grid_rows + halo, LANE)
    split_proc = round_up(nodes + halo, LANE)
    total_enc = round_up(split_enc + nodes, LANE)
    total_proc = round_up(split_proc + nodes, LANE)
    sizes = (grid_rows, nodes, enc_edges, slots_total, lat, tile, halo, split_enc, total_enc, split_proc, total_proc)
    stages = n.bit_length() - 1
    large = [grid_latent, mesh_latent, g2m_latent, edge_latent, cotangent, *weights]
    small = [
        grid_send.reshape(halo, 1), node_send.reshape(halo, 1), node_send,
        g2m_sender.reshape(-1, 1, tile), g2m_receiver.reshape(-1, 1, tile),
        edge_sender.reshape(-1, 1, tile), edge_receiver.reshape(-1, 1, tile), gains, biases,
    ]
    in_vmem = pl.BlockSpec(memory_space=pltpu.VMEM)
    scratch = [pltpu.VMEM(a.shape, a.dtype) for a in large]
    scratch += [
        pltpu.VMEM((total_enc, lat), BF16),
        pltpu.VMEM((total_proc, lat), BF16),
        pltpu.VMEM((nodes + halo, lat), BF16),
        pltpu.VMEM((nodes, lat), F32),
        pltpu.VMEM((slots_total, lat), F32),
        pltpu.VMEM((slots_total, lat), F32),
        pltpu.VMEM((slots_total, LANE), F32),
        pltpu.VMEM((slots_total, lat), BF16),
        pltpu.VMEM((slots_total, lat), BF16),
        pltpu.VMEM((slots_total, lat), BF16),
        pltpu.VMEM((total_proc, lat), F32),
        pltpu.VMEM((nodes, lat), F32),
        pltpu.VMEM((3, halo * lat // LANE, LANE), F32),
        pltpu.VMEM((3, halo * lat // LANE, LANE), F32),
        pltpu.SemaphoreType.DMA((13,)),
        pltpu.SemaphoreType.DMA((3,)),
        pltpu.SemaphoreType.DMA((3,)),
    ]
    if inside:
        scratch += [pltpu.VMEM((UNITS, lat, lat), F32)]
        for dtype in (F32, BF16, BF16):
            scratch += [pltpu.VMEM((UNITS, lat >> (k + 1), lat), dtype) for k in range(stages)]
        scratch += [pltpu.SemaphoreType.DMA((UNITS, stages)), pltpu.SemaphoreType.DMA((UNITS, stages))]
    mesh_out, grad_mesh, grads = pl.pallas_call(
        functools.partial(kernel, n, inside, sizes),
        out_shape=(
            jax.ShapeDtypeStruct((nodes, lat), BF16),
            jax.ShapeDtypeStruct((nodes, lat), F32),
            jax.ShapeDtypeStruct((UNITS, lat // n if inside else lat, lat), F32),
        ),
        in_specs=[pl.BlockSpec(memory_space=pl.ANY)] * 13 + [pl.BlockSpec(memory_space=pltpu.SMEM)] + [in_vmem] * len(small),
        out_specs=(in_vmem, in_vmem, in_vmem),
        scratch_shapes=scratch,
        compiler_params=pltpu.CompilerParams(collective_id=0, has_side_effects=True, vmem_limit_bytes=60 * 1024 * 1024),
    )(*large, edge_count, *small)
    if not inside:
        grads = lax.psum_scatter(grads, "band", scatter_dimension=1, tiled=True)
    edge_scale = 1.0 / (slots_total * n) ** 0.5
    node_scale = 1.0 / (nodes * n) ** 0.5

    def shard(first, count, scale):
        return jnp.transpose(grads[first:first + count], (0, 2, 1)).reshape(count * lat, lat // n) * scale

    return (mesh_out, grad_mesh, shard(4, 3, edge_scale), shard(3, 1, edge_scale), shard(1, 2, node_scale), shard(0, 1, node_scale))


def solution(mesh):
    rows = P(("member", "band"), None)
    placed = (rows,) * 5 + (P("band", None), P("band"), P("band"), P("band", None), P("band"), P("band"), P("band")) + (P(),) * 10
    shard = P("member", "band")
    return jax.shard_map(
        functools.partial(on_device, mesh.shape["band"]),
        mesh=mesh,
        in_specs=placed,
        out_specs=(rows, rows, shard, shard, shard, shard),
        check_vma=False,
    )
```

```python
import functools

import jax
import jax.numpy as jnp
from jax import lax
from jax.experimental import pallas as pl
from jax.experimental.pallas import tpu as pltpu
from jax.sharding import PartitionSpec as P

EPS = 1e-05
F32 = jnp.float32
BF16 = jnp.bfloat16
UNITS = 7
LANE = 128


def round_up(value, step):
    return (value + step - 1) // step * step


def nn(a, b):
    return jnp.dot(a, b, preferred_element_type=F32)


def nt(a, b):
    return lax.dot_general(a, b, (((1,), (1,)), ((), ())), preferred_element_type=F32)


def tn(a, b):
    return lax.dot_general(a, b, (((0,), (0,)), ((), ())), preferred_element_type=F32)


def sigmoid(a):
    return 0.5 * jnp.tanh(0.5 * a) + 0.5


def silu_slope(a):
    s = sigmoid(a)
    return s * (1.0 + a * (1.0 - s))


def normalise(linear):
    centred = linear - jnp.mean(linear, axis=-1, keepdims=True)
    inverse = lax.rsqrt(jnp.mean(centred * centred, axis=-1, keepdims=True) + EPS)
    return centred * inverse, inverse


def norm_back(z, inverse, scaled):
    return inverse * (
        scaled
        - jnp.mean(scaled, axis=-1, keepdims=True)
        - z * jnp.mean(scaled * z, axis=-1, keepdims=True)
    )


def hot_rows(index_row, rows_total, first=0):
    edges = index_row.shape[1]
    ids = lax.broadcasted_iota(jnp.int32, (rows_total, edges), 0) + first
    return jnp.where(ids == index_row, 1.0, 0.0).astype(BF16)


def over_lanes(index_row):
    edges = index_row.shape[1]
    return jnp.transpose(jnp.broadcast_to(index_row.astype(F32), (LANE, edges)))


def hot_pair(sender_row, receiver_row, split, total):
    edges = sender_row.shape[1]
    ids = lax.broadcasted_iota(jnp.int32, (edges, LANE), 1).astype(F32)
    senders, receivers = over_lanes(sender_row), over_lanes(receiver_row)
    blocks = []
    for start in range(0, total, LANE):
        held = senders if start < split else receivers
        offset = start if start < split else start - split
        blocks.append(jnp.where(held == ids + float(offset), 1.0, 0.0).astype(BF16))
    return jnp.concatenate(blocks, axis=1)


def kernel(n, inside, sizes, *refs):
    (grid_rows, nodes, enc_edges, slots_total, lat, tile, halo, split_enc, total_enc, split_proc, total_proc) = sizes
    stages = n.bit_length() - 1
    refs = list(refs)
    hbm = refs[:13]
    (count_ref, gsend_row, nsend_row, g2m_s, g2m_r, edge_s, edge_r, gains, biases) = refs[13:22]
    mesh_out_ref, grad_mesh_ref = refs[22:24]
    outs, refs = refs[24:28 if inside else 25], refs[28 if inside else 25:]
    vm = refs[:13]
    (table_enc, table_proc, node_table, acc_node, pre_ref, z_ref, inv_ref, hid_ref, elg_ref, epg_ref,
     sum_ref, upd_ref, a_send, a_recv, in_sem, a_ssem, a_rsem) = refs[13:30]
    rest = refs[30:]
    if inside:
        full_ref, keep, send, recv, r_ssem, r_rsem = (
            rest[0], rest[1:1 + stages], rest[1 + stages:1 + 2 * stages], rest[1 + 2 * stages:1 + 3 * stages],
            rest[1 + 3 * stages], rest[2 + 3 * stages])
    else:
        full_ref = outs[0]
    me = lax.axis_index("band")

    barrier = pltpu.get_barrier_semaphore()

    def greet(step, carry):
        pl.semaphore_signal(barrier, inc=1, device_id={"band": lax.rem(me + step, n)}, device_id_type=pl.DeviceIdType.MESH)
        return carry

    copies = [pltpu.make_async_copy(hbm[i], vm[i], in_sem.at[i]) for i in range(13)]
    (GRID, MESH, G2M, EDGE, COT, EEI, EEO, ENI, ENO, PEI, PEO, PNI, PNO) = range(13)
    for i in (GRID, EEI, MESH, G2M, EEO, ENI, ENO, PEI, EDGE, PEO, PNI, PNO, COT):
        copies[i].start()
    lax.fori_loop(1, n, greet, 0)

    rows_block = halo * lat // LANE // n
    spread = lat // LANE

    def exchange_fill(which, rows):
        for c in range(spread):
            a_send[which, pl.ds(c, halo, stride=spread), :] = rows[:, c * LANE:(c + 1) * LANE]

    def exchange_start(which):
        own = pl.ds(pl.multiple_of(me * rows_block, rows_block), rows_block)
        a_recv[which, own, :] = a_send[which, own, :]

        def go(step, carry):
            peer = lax.rem(me + step, n)
            pltpu.make_async_remote_copy(
                src_ref=a_send.at[which, pl.ds(pl.multiple_of(peer * rows_block, rows_block), rows_block)],
                dst_ref=a_recv.at[which, own],
                send_sem=a_ssem.at[which],
                recv_sem=a_rsem.at[which],
                device_id={"band": peer},
                device_id_type=pl.DeviceIdType.MESH,
            ).start()
            return carry

        lax.fori_loop(1, n, go, 0)

    def exchange_wait(which):
        most = pl.ds(0, (n - 1) * rows_block)
        pltpu.make_async_copy(a_send.at[which, most], a_recv.at[which, most], a_rsem.at[which]).wait()
        pltpu.make_async_copy(a_send.at[which, most], a_recv.at[which, most], a_ssem.at[which]).wait()
        return jnp.concatenate([a_recv[which, pl.ds(c, halo, stride=spread), :] for c in range(spread)], axis=1).astype(BF16)

    block = lat // n
    if inside:
        bits = [lax.rem(lax.div(me, jnp.int32(1 << k)), jnp.int32(2)) for k in range(stages)]

    def remote(units, k):
        first, count, order, _ = units
        bit = order[k]
        return pltpu.make_async_remote_copy(
            src_ref=send[k].at[pl.ds(first, count)],
            dst_ref=recv[k].at[pl.ds(first, count)],
            send_sem=r_ssem.at[first, k],
            recv_sem=r_rsem.at[first, k],
            device_id={"band": me + (1 - 2 * bits[bit]) * (1 << bit)},
            device_id_type=pl.DeviceIdType.MESH,
        )

    def reduce_step(units, k):
        if not inside:
            return
        first, count, order, place = units
        us = pl.ds(first, count)

        def value(j):
            rows = pl.ds(pl.multiple_of(j * block, block), block)
            if k == 0:
                return full_ref[us, rows, :]
            return keep[k - 1][us, rows, :] + recv[k - 1][us, rows, :].astype(F32)

        if k > 0:
            remote(units, k - 1).wait_recv()
        if k == stages:
            total = value(0)
            for unit in range(count):
                which, column, scale = place[unit]
                outs[which][:, column * lat:(column + 1) * lat] = total[unit] * scale
            return
        at = sorted(order[k:]).index(order[k])
        bit = bits[order[k]]

        def whole(j, chosen):
            return ((j >> at) << (at + 1)) + (j & ((1 << at) - 1)) + chosen * (1 << at)

        for j in range(n >> (k + 1)):
            send[k][us, j * block:(j + 1) * block, :] = value(whole(j, 1 - bit)).astype(BF16)
        remote(units, k).start()
        for j in range(n >> (k + 1)):
            keep[k][us, j * block:(j + 1) * block, :] = value(whole(j, bit))

    low_first, high_first = (0, 1, 2, 3), (0, 2, 3, 1)
    edge_scale = 1.0 / (slots_total * n) ** 0.5
    node_scale = 1.0 / (nodes * n) ** 0.5
    N0 = (0, 1, high_first, ((3, 0, node_scale),))
    N12 = (1, 2, low_first, ((2, 0, node_scale), (2, 1, node_scale)))
    EOUT = (3, 1, low_first, ((1, 0, edge_scale),))
    E4 = (4, 1, low_first, ((0, 0, edge_scale),))
    E5 = (5, 1, high_first, ((0, 1, edge_scale),))
    E6 = (6, 1, low_first, ((0, 2, edge_scale),))

    copies[GRID].wait()
    grid = vm[GRID]
    exchange_fill(0, tn(hot_rows(gsend_row[...], grid_rows), grid[...]))
    copies[EEI].wait()
    copies[MESH].wait()
    eei = vm[EEI]
    mesh = vm[MESH]
    table_enc[0:grid_rows, :] = nn(grid[...], eei[0:lat, :]).astype(BF16)
    table_enc[split_enc:split_enc + nodes, :] = nn(mesh[...], eei[lat:2 * lat, :]).astype(BF16)
    if split_enc > grid_rows + halo:
        table_enc[grid_rows + halo:split_enc, :] = jnp.zeros((split_enc - grid_rows - halo, lat), BF16)
    if total_enc > split_enc + nodes:
        table_enc[split_enc + nodes:total_enc, :] = jnp.zeros((total_enc - split_enc - nodes, lat), BF16)
    if split_proc > nodes + halo:
        table_proc[nodes + halo:split_proc, :] = jnp.zeros((split_proc - nodes - halo, lat), BF16)
    if total_proc > split_proc + nodes:
        table_proc[split_proc + nodes:total_proc, :] = jnp.zeros((total_proc - split_proc - nodes, lat), BF16)
    table_enc[grid_rows:grid_rows + halo, :] = jnp.zeros((halo, lat), BF16)
    pl.semaphore_wait(barrier, n - 1)
    exchange_start(0)
    copies[G2M].wait()

    def index_row(ref, t):
        return ref[pl.ds(t * tile, tile)].reshape(1, tile)

    def encode_local(t):
        rows = pl.ds(t * tile, tile)
        pre = nn(hot_pair(index_row(g2m_s, t), index_row(g2m_r, t), split_enc, total_enc), table_enc[...])
        pre_ref[rows, :] = pre + nn(vm[G2M][rows, :], eei[2 * lat:3 * lat, :])

    for t in range(enc_edges // tile):
        encode_local(t)
    copies[EEO].wait()
    copies[ENI].wait()
    acc_node[...] = jnp.zeros_like(acc_node)
    upd_ref[...] = nn(mesh[...], vm[ENI][0:lat, :])

    def hot_halo(senders, first, rows_local):
        held = over_lanes(senders)
        ids = lax.broadcasted_iota(jnp.int32, (tile, LANE), 1).astype(F32)
        blocks = [jnp.where(held == ids + float(start), 1.0, 0.0).astype(BF16) for start in range(first, rows_local, LANE)]
        return blocks[0] if len(blocks) == 1 else jnp.concatenate(blocks, axis=1)

    def halo_rows(own_rows, split, arrived_rows):
        first = own_rows // LANE * LANE
        parts = [arrived_rows]
        if own_rows > first:
            parts = [jnp.zeros((own_rows - first, lat), BF16)] + parts
        if split > own_rows + halo:
            parts = parts + [jnp.zeros((split - own_rows - halo, lat), BF16)]
        return parts[0] if len(parts) == 1 else jnp.concatenate(parts, axis=0)

    arrived = exchange_wait(0)
    far = halo_rows(grid_rows, split_enc, nn(arrived, eei[0:lat, :]).astype(BF16))

    def encode(t):
        rows = pl.ds(t * tile, tile)
        pre = pre_ref[rows, :] + nn(hot_halo(index_row(g2m_s, t), grid_rows // LANE * LANE, split_enc), far)
        hidden = (pre * sigmoid(pre)).astype(BF16)
        z, _ = normalise(nn(hidden, vm[EEO][...]))
        message = (z * gains[0:1, :] + biases[0:1, :]).astype(BF16)
        acc_node[...] += nn(hot_rows(index_row(g2m_r, t), nodes), message)

    for t in range(enc_edges // tile):
        encode(t)
    copies[ENO].wait()
    pre = upd_ref[...] + nn(acc_node[...].astype(BF16), vm[ENI][lat:2 * lat, :])
    hidden = (pre * sigmoid(pre)).astype(BF16)
    z, _ = normalise(nn(hidden, vm[ENO][...]))
    encoded = (mesh[...].astype(F32) + z * gains[1:2, :] + biases[1:2, :]).astype(BF16)
    node_table[0:nodes, :] = encoded
    exchange_fill(1, tn(hot_rows(nsend_row[...], nodes), encoded))
    exchange_start(1)

    copies[PEI].wait()
    copies[EDGE].wait()
    copies[PEO].wait()
    copies[PNI].wait()
    pei, pni = vm[PEI], vm[PNI]
    table_proc[0:nodes, :] = nn(encoded, pei[0:lat, :]).astype(BF16)
    table_proc[split_proc:split_proc + nodes, :] = nn(encoded, pei[lat:2 * lat, :]).astype(BF16)
    table_proc[nodes:nodes + halo, :] = jnp.zeros((halo, lat), BF16)
    count = count_ref[0]

    def live_rows(ref, t):
        slot = lax.broadcasted_iota(jnp.int32, (1, tile), 1) + t * tile
        return jnp.where(slot < count, ref[t], -1)

    def process_local(t):
        rows = pl.ds(t * tile, tile)
        pre = nn(hot_pair(live_rows(edge_s, t), live_rows(edge_r, t), split_proc, total_proc), table_proc[...])
        pre_ref[rows, :] = pre + nn(vm[EDGE][rows, :], pei[2 * lat:3 * lat, :])

    for t in range(slots_total // tile):
        process_local(t)
    upd_ref[...] = nn(encoded, pni[0:lat, :])
    acc_node[...] = jnp.zeros_like(acc_node)
    arrived = exchange_wait(1)
    node_table[nodes:nodes + halo, :] = arrived
    far = halo_rows(nodes, split_proc, nn(arrived, pei[0:lat, :]).astype(BF16))

    def process(t):
        rows = pl.ds(t * tile, tile)
        pre = pre_ref[rows, :] + nn(hot_halo(live_rows(edge_s, t), nodes // LANE * LANE, split_proc), far)
        pre_ref[rows, :] = pre
        hidden = (pre * sigmoid(pre)).astype(BF16)
        hid_ref[rows, :] = hidden
        z, inverse = normalise(nn(hidden, vm[PEO][...]))
        z_ref[rows, :] = z
        inv_ref[rows, :] = jnp.broadcast_to(inverse, (tile, LANE))
        message = (z * gains[2:3, :] + biases[2:3, :]).astype(BF16)
        acc_node[...] += nn(hot_rows(live_rows(edge_r, t), nodes), message)

    for t in range(slots_total // tile):
        process(t)

    proc_sum = acc_node[...].astype(BF16)
    copies[PNO].wait()
    copies[COT].wait()
    pno, cot = vm[PNO], vm[COT]
    pre = upd_ref[...] + nn(proc_sum, pni[lat:2 * lat, :])
    hidden = (pre * sigmoid(pre)).astype(BF16)
    z, inverse = normalise(nn(hidden, pno[...]))
    mesh_out_ref[...] = (encoded.astype(F32) + z * gains[3:4, :] + biases[3:4, :]).astype(BF16)
    lin_grad = norm_back(z, inverse, cot[...].astype(F32) * gains[3:4, :]).astype(BF16)
    full_ref[0, :, :] = tn(lin_grad, hidden)
    reduce_step(N0, 0)
    pre_grad = (nt(lin_grad, pno[...]) * silu_slope(pre)).astype(BF16)
    full_ref[1, :, :] = tn(pre_grad, encoded)
    full_ref[2, :, :] = tn(pre_grad, proc_sum)
    reduce_step(N12, 0)
    sum_grad = nt(pre_grad, pni[lat:2 * lat, :]).astype(BF16)
    grad_mesh_ref[...] = cot[...].astype(F32) + nt(pre_grad, pni[0:lat, :])
    if split_proc + nodes < total_proc:
        table_proc[split_proc + nodes:total_proc, :] = jnp.zeros((total_proc - split_proc - nodes, lat), BF16)
    table_proc[split_proc:split_proc + nodes, :] = sum_grad
    sum_ref[...] = jnp.zeros_like(sum_ref)

    def edge_back(t):
        rows = pl.ds(t * tile, tile)
        senders, receivers = live_rows(edge_s, t), live_rows(edge_r, t)
        held = over_lanes(receivers)
        ids = lax.broadcasted_iota(jnp.int32, (tile, LANE), 1).astype(F32)
        hot = jnp.concatenate(
            [jnp.where(held == ids + float(s), 1.0, 0.0).astype(BF16) for s in range(0, total_proc - split_proc, LANE)], axis=1)
        upstream = nn(hot, table_proc[split_proc:total_proc, :])
        grad = norm_back(z_ref[rows, :], inv_ref[rows, 0:1], upstream * gains[2:3, :]).astype(BF16)
        elg_ref[rows, :] = grad
        grad = (nt(grad, vm[PEO][...]) * silu_slope(pre_ref[rows, :])).astype(BF16)
        epg_ref[rows, :] = grad
        sum_ref[0:split_proc, :] += nn(hot_rows(senders, split_proc), grad)
        sum_ref[split_proc:split_proc + nodes, :] += nn(hot_rows(receivers, nodes), grad)

    for t in range(slots_total // tile):
        edge_back(t)
        if t == 0:
            reduce_step(N0, 1)
            reduce_step(N12, 1)
    by_sender = sum_ref[0:nodes + halo, :].astype(BF16)
    by_receiver = sum_ref[split_proc:split_proc + nodes, :].astype(BF16)
    exchange_fill(2, nt(by_sender[nodes:nodes + halo, :], pei[0:lat, :]))
    exchange_start(2)
    full_ref[3, :, :] = tn(elg_ref[...], hid_ref[...])
    reduce_step(EOUT, 0)
    full_ref[5, :, :] = tn(by_receiver, node_table[0:nodes, :])
    reduce_step(E5, 0)
    reduce_step(N0, 2)
    full_ref[6, :, :] = tn(epg_ref[...], vm[EDGE][...])
    reduce_step(E6, 0)
    reduce_step(EOUT, 1)
    reduce_step(E5, 1)
    full_ref[4, :, :] = tn(by_sender, node_table[...])
    reduce_step(E4, 0)
    reduce_step(N12, 2)
    reduce_step(E6, 1)
    reduce_step(N0, 3)
    grad_mesh_ref[...] += nt(by_sender[0:nodes, :], pei[0:lat, :]) + nt(by_receiver, pei[lat:2 * lat, :])
    reduce_step(E4, 1)
    arrived = exchange_wait(2)
    grad_mesh_ref[...] += nn(hot_rows(nsend_row[...], nodes), arrived)
    reduce_step(N0, 4)
    reduce_step(EOUT, 2)
    reduce_step(E5, 2)
    reduce_step(N12, 3)
    reduce_step(E6, 2)
    reduce_step(EOUT, 3)
    reduce_step(E5, 3)
    reduce_step(N12, 4)
    reduce_step(E4, 2)
    reduce_step(EOUT, 4)
    reduce_step(E6, 3)
    reduce_step(E5, 4)
    reduce_step(E4, 3)
    reduce_step(E6, 4)
    reduce_step(E4, 4)
    if inside:
        for units in (N0, N12, EOUT, E4, E5, E6):
            for k in range(stages):
                remote(units, k).wait_send()


def on_device(n, *args):
    (grid_latent, mesh_latent, g2m_latent, edge_latent, cotangent, grid_send, g2m_sender, g2m_receiver, node_send,
     edge_sender, edge_receiver, edge_count, *weights) = args
    weights, (gains, biases) = weights[:8], weights[8:]
    lat = mesh_latent.shape[1]
    grid_rows, nodes = grid_latent.shape[0], mesh_latent.shape[0]
    enc_edges, slots_total = g2m_latent.shape[0], edge_latent.shape[0]
    halo = node_send.shape[1]
    tile = 256
    inside = n == 16
    split_enc = round_up(grid_rows + halo, LANE)
    split_proc = round_up(nodes + halo, LANE)
    total_enc = round_up(split_enc + nodes, LANE)
    total_proc = round_up(split_proc + nodes, LANE)
    sizes = (grid_rows, nodes, enc_edges, slots_total, lat, tile, halo, split_enc, total_enc, split_proc, total_proc)
    stages = n.bit_length() - 1
    large = [grid_latent, mesh_latent, g2m_latent, edge_latent, cotangent, *weights]
    small = [
        grid_send, node_send, g2m_sender, g2m_receiver,
        edge_sender.reshape(-1, 1, tile), edge_receiver.reshape(-1, 1, tile), gains, biases,
    ]
    in_vmem = pl.BlockSpec(memory_space=pltpu.VMEM)
    scratch = [pltpu.VMEM(a.shape, a.dtype) for a in large]
    scratch += [
        pltpu.VMEM((total_enc, lat), BF16),
        pltpu.VMEM((total_proc, lat), BF16),
        pltpu.VMEM((nodes + halo, lat), BF16),
        pltpu.VMEM((nodes, lat), F32),
        pltpu.VMEM((slots_total, lat), F32),
        pltpu.VMEM((slots_total, lat), F32),
        pltpu.VMEM((slots_total, LANE), F32),
        pltpu.VMEM((slots_total, lat), BF16),
        pltpu.VMEM((slots_total, lat), BF16),
        pltpu.VMEM((slots_total, lat), BF16),
        pltpu.VMEM((total_proc, lat), F32),
        pltpu.VMEM((nodes, lat), F32),
        pltpu.VMEM((3, halo * lat // LANE, LANE), F32),
        pltpu.VMEM((3, halo * lat // LANE, LANE), F32),
        pltpu.SemaphoreType.DMA((13,)),
        pltpu.SemaphoreType.DMA((3,)),
        pltpu.SemaphoreType.DMA((3,)),
    ]
    if inside:
        scratch += [pltpu.VMEM((UNITS, lat, lat), F32)]
        for dtype in (F32, BF16, BF16):
            scratch += [pltpu.VMEM((UNITS, lat >> (k + 1), lat), dtype) for k in range(stages)]
        scratch += [pltpu.SemaphoreType.DMA((UNITS, stages)), pltpu.SemaphoreType.DMA((UNITS, stages))]
    if inside:
        grad_shapes = [jax.ShapeDtypeStruct((lat // n, width * lat), F32) for width in (3, 1, 2, 1)]
    else:
        grad_shapes = [jax.ShapeDtypeStruct((UNITS, lat, lat), F32)]
    mesh_out, grad_mesh, *grads = pl.pallas_call(
        functools.partial(kernel, n, inside, sizes),
        out_shape=(
            jax.ShapeDtypeStruct((nodes, lat), BF16),
            jax.ShapeDtypeStruct((nodes, lat), F32),
            *grad_shapes,
        ),
        in_specs=[pl.BlockSpec(memory_space=pl.ANY)] * 13 + [pl.BlockSpec(memory_space=pltpu.SMEM)] + [in_vmem] * len(small),
        out_specs=(in_vmem,) * (2 + len(grad_shapes)),
        scratch_shapes=scratch,
        compiler_params=pltpu.CompilerParams(collective_id=0, has_side_effects=True, vmem_limit_bytes=60 * 1024 * 1024),
    )(*large, edge_count, *small)
    if inside:
        return (mesh_out, grad_mesh, *(jnp.transpose(g) for g in grads))
    grads = lax.psum_scatter(grads[0], "band", scatter_dimension=1, tiled=True)
    edge_scale = 1.0 / (slots_total * n) ** 0.5
    node_scale = 1.0 / (nodes * n) ** 0.5

    def shard(first, count, scale):
        return jnp.transpose(grads[first:first + count], (0, 2, 1)).reshape(count * lat, lat // n) * scale

    return (mesh_out, grad_mesh, shard(4, 3, edge_scale), shard(3, 1, edge_scale), shard(1, 2, node_scale), shard(0, 1, node_scale))


def solution(mesh):
    rows = P(("member", "band"), None)
    placed = (rows,) * 5 + (P("band", None), P("band"), P("band"), P("band", None), P("band"), P("band"), P("band")) + (P(),) * 10
    shard = P("member", "band")
    return jax.shard_map(
        functools.partial(on_device, mesh.shape["band"]),
        mesh=mesh,
        in_specs=placed,
        out_specs=(rows, rows, shard, shard, shard, shard),
        check_vma=False,
    )
```
